32 devices in a mesh: grp: 2 (over y), ex: 8 (over z, x), feat: 2 (over core).
Axes of the slice: x: 2, y: 2, z: 4, core: 2. Of those that a mesh axis runs over, the one named last changes fastest.
Arguments:
- slab_one: bfloat16 [4096, 4096], P(('grp', 'ex'), 'feat'), parts along dimension 0, may hold values from -6 to 6
- slab_two: bfloat16 [4096, 4096], P(('grp', 'ex'), 'feat'), parts along dimension 0, may hold values from -6 to 6
- target_product: bfloat16 [4096, 2048], P('feat', 'grp'), parts along dimension 1, may hold values from -0.09375 to 0.09375
Outputs:
- kernel_diag: float32 [2, 4096, 2048], P('feat', ('grp', 'ex')), parts along dimension 1
- kernel_cross: float32 [4096, 2048], P(('grp', 'ex', 'feat')), parts along dimension 0
- scores: bfloat16 [2, 4096, 1024], P(None, ('grp', 'ex'), 'feat'), parts along dimension 1
The draws below stay inside these ranges and needn't reach their ends.
There are 2 independent parts, one for each index of `grp`. The reference program is written for one: setup_inputs(seed, part) draws one part's arguments, and reference() takes and returns one part's arrays. A program takes and returns all parts, laid end to end along the dimension named above; each array names one. Nothing has to cross between parts.
All inputs are finite; a program needn't handle non-finite values.
Results may differ from the reference program's by a relative error of at most 0.0004.
Values may be sent and summed in bfloat16 or wider, within the bound.
No kernel may reach another device: no remote copies, remote signals or barrier semaphores. Data moves between devices by JAX's collectives and lax.ppermute only.
A program may use at most 128 MiB of HBM per device.

```python
import math
import jax
import jax.numpy as jnp

P_SIZE = 4096
TGT = 1024
ROWS = 2048


def block_scale(rng, dims, cuts, low, largest):
    def one(axis_at, parts):
        steps = jax.random.uniform(jax.random.fold_in(jax.random.fold_in(rng, 6), axis_at), (parts,), jnp.float32, low / len(cuts), largest / len(cuts))
        return jnp.repeat(jnp.exp(steps), dims[axis_at] // parts).reshape((-1,) + (1,) * (len(dims) - axis_at - 1))

    level = one(*cuts[0])
    for cut in cuts[1:]:
        level = level * one(*cut)
    return level


def scatter_about(rng, shape, scale, bound, pieces=(), kind=jnp.bfloat16):
    values = scale * jax.random.normal(rng, shape, jnp.float32)
    if pieces:
        values = values * block_scale(rng, shape, pieces, -0.22, 0.18)
    return jnp.clip(values, -bound, bound).astype(kind)


def setup_inputs(seed: int = 0, part: int = 0) -> dict:
    key_of = jax.random.split(jax.random.key(seed), 4)
    own_keys = jax.random.split(jax.random.fold_in(key_of[3], part), 4)
    slab_one = scatter_about(own_keys[0], (ROWS, P_SIZE), 1.0, 6.0, ((0, 8), (1, 2)))
    slab_two = scatter_about(own_keys[1], (ROWS, P_SIZE), 1.0, 6.0, ((0, 8), (1, 2)))
    target_product = scatter_about(own_keys[2], (P_SIZE, TGT), P_SIZE ** -0.5, 0.09375, ((0, 2),))
    return dict(slab_one=slab_one, slab_two=slab_two, target_product=target_product)


def reference(slab_one, slab_two, target_product):
    half_width = P_SIZE // 2
    factor = 1.0 / math.sqrt(ROWS)
    blocks = []
    for block in range(2):
        lower = block * half_width
        total = jnp.zeros((half_width, half_width), jnp.float32)
        for slab_piece in (slab_one, slab_two):
            columns = slab_piece[:, lower:lower + half_width]
            total = total + jnp.dot(columns.T, columns, preferred_element_type=jnp.float32)
        blocks.append(total * factor)
    kernel_diag = jnp.stack(blocks)
    cross = jnp.zeros((half_width, half_width), jnp.float32)
    for slab_piece in (slab_one, slab_two):
        cross = cross + jnp.dot(slab_piece[:, :half_width].T, slab_piece[:, half_width:], preferred_element_type=jnp.float32)
    kernel_cross = cross * factor
    scores = jnp.stack([jnp.dot(slab_one, target_product, preferred_element_type=jnp.float32), jnp.dot(slab_two, target_product, preferred_element_type=jnp.float32)]).astype(jnp.bfloat16)
    return (kernel_diag, kernel_cross, scores)
```

```python
import math

import jax
import jax.numpy as jnp
from jax import lax
from jax.sharding import PartitionSpec as P


def gram_part(left, right):
    return lax.dot_general(
        left, right, (((0,), (0,)), ((), ())), preferred_element_type=jnp.float32
    )


def reducing(slab_one, slab_two, target_product):
    ex_devices = lax.axis_size("ex")
    feat_devices = lax.axis_size("feat")
    row_count, half_width = slab_one.shape
    factor = 1.0 / math.sqrt(row_count * ex_devices)
    feat_index = lax.axis_index("feat")
    cross_width = half_width // (ex_devices * feat_devices)
    gathered_one, gathered_two = (
        lax.all_gather(slab_one, "feat", axis=1, tiled=True),
        lax.all_gather(slab_two, "feat", axis=1, tiled=True),
    )
    total = gram_part(slab_one, slab_one) + gram_part(slab_two, slab_two)
    diag_rows = lax.psum_scatter(total * factor, "ex", scatter_dimension=0, tiled=True)
    kernel_diag = diag_rows[None]

    def select_columns(gathered):
        first_half = gathered[:, :half_width].reshape(
            row_count, ex_devices, feat_devices, cross_width
        )
        chosen = lax.dynamic_index_in_dim(first_half, feat_index, 2, keepdims=False)
        return chosen.reshape(row_count, ex_devices * cross_width)

    total = gram_part(select_columns(gathered_one), gathered_one[:, half_width:])
    total = total + gram_part(select_columns(gathered_two), gathered_two[:, half_width:])
    kernel_cross = lax.psum_scatter(total * factor, "ex", scatter_dimension=0, tiled=True)
    target_half = lax.all_to_all(target_product, "feat", split_axis=1, concat_axis=0, tiled=True)
    scores = jnp.stack(
        [
            jnp.dot(gathered_one, target_half, preferred_element_type=jnp.float32),
            jnp.dot(gathered_two, target_half, preferred_element_type=jnp.float32),
        ]
    ).astype(jnp.bfloat16)
    return (kernel_diag, kernel_cross, scores)


Z, X = 4, 2


def permute(value, moves):
    pairs = [
        ((fz * X + x) * 2 + fc, (tz * X + x) * 2 + tc)
        for (fz, fc), (tz, tc) in moves
        for x in range(X)
    ]
    return lax.ppermute(value, ("ex", "feat"), pairs)


def swap_x(value, holders):
    pairs = [
        ((z * X + x) * 2 + c, (z * X + 1 - x) * 2 + c) for z, c in holders for x in range(X)
    ]
    return lax.ppermute(value, ("ex", "feat"), pairs)


def swap_core(value):
    return lax.ppermute(value, "feat", [(0, 1), (1, 0)])


ENDS = ((0, 1), (3, 2))


def on_core(core, moves):
    return [((f, core), (t, core)) for f, t in moves]


IN = [(e, c) for e, c in ENDS]
OUT = [(c, e) for e, c in ENDS]
MID = [(1, 2), (2, 1)]
OVER = [(0, 2), (3, 1)]
HOLDERS = [(0, 1), (1, 0), (1, 1), (2, 0), (2, 1), (3, 1)]


def gathering(slab_one, slab_two, target_product):
    row_count, width = slab_one.shape
    factor = 1.0 / math.sqrt(row_count * Z * X)
    core = lax.axis_index("feat")
    ex = lax.axis_index("ex")
    z, x = ex // X, ex % X
    upper = z // 2
    centre = (z == 1) | (z == 2)
    group = width // Z
    half = width // 2
    block = width // (Z * X)

    def columns(half_index):
        return jnp.concatenate(
            [
                lax.dynamic_slice_in_dim(s, half_index * half, half, 1)
                for s in (slab_one, slab_two)
            ],
            0,
        )

    near, far = columns(upper), columns(1 - upper)

    a_moves = on_core(0, IN) + on_core(1, IN + OUT)
    b0n = permute(far, on_core(0, MID))
    c0n = permute(far, on_core(0, OVER))
    an = permute(near, a_moves)
    b1n = permute(far, on_core(1, MID))
    c1n = permute(far, on_core(1, OVER))
    af = permute(far, a_moves)
    b0f = permute(near, on_core(0, MID))
    c0f = permute(near, on_core(0, OVER))
    b1f = permute(near, on_core(1, MID))
    c1f = permute(near, on_core(1, OVER))

    targets = target_product.shape[1]
    half_targets = targets // 2

    def partial_scores(which):
        t = lax.dynamic_slice_in_dim(target_product, which * half_targets, half_targets, 1)
        return jnp.concatenate(
            [jnp.dot(s, t, preferred_element_type=jnp.float32) for s in (slab_one, slab_two)], 0
        )

    other_scores = swap_core(partial_scores(1 - core))
    scores = (partial_scores(core) + other_scores).astype(jnp.bfloat16)
    scores = scores.reshape(2, row_count, half_targets)

    mine = (z % 2) * group
    theirs = (1 - z % 2) * group

    def cut(value, start, size):
        return lax.dynamic_slice_in_dim(value, start, size, 1)

    given = permute(
        jnp.concatenate([cut(v, theirs, group) for v in (near, b0n, c0n)], 0),
        [((c, 0), (e, 1)) for e, c in ENDS],
    )
    across = lax.ppermute(
        jnp.concatenate([cut(v, mine, group) for v in (near, an, b0n, c0n)], 0),
        "feat",
        [(0, 1)],
    )
    rows = 2 * row_count
    first_block = jnp.concatenate(
        [across[:rows], jnp.where(centre, across[rows:], given)], 0
    )

    def arrived(core_zero, core_one, forwarded):
        return jnp.where(core == 0, core_zero, jnp.where(centre, core_one, forwarded))

    def gathered(own, a, b0, b1, c0, c1):
        db = permute(b1, on_core(1, OUT))
        dc = permute(c1, on_core(1, OUT))
        return jnp.concatenate([own, a, arrived(b0, b1, db), arrived(c0, c1, dc)], 0)

    all_near = gathered(near, an, b0n, b1n, c0n, c1n)

    def left(which):
        u = cut(all_near, mine + which * block, block)
        v = jnp.where(
            core == 0,
            cut(all_near, theirs + which * block, block),
            cut(first_block, which * block, block),
        )
        return jnp.concatenate([u, v], 1)

    left_other, left_mine = left(1 - x), left(x)

    def finish(right):
        other = swap_x(gram_part(left_other, right), HOLDERS)
        total = (gram_part(left_mine, right) + other) * factor
        end_diag = permute(total[block:], on_core(0, OUT))
        low_cross = lax.ppermute(total[block : block + block // 2], "feat", [(1, 0)])
        diag = jnp.where((core == 0) & ~centre, end_diag, total[:block])
        cross = jnp.where(core == 0, low_cross, total[block + block // 2 :])
        return diag, cross

    near_out = finish(all_near)
    all_far = gathered(far, af, b0f, b1f, c0f, c1f)
    far_out = finish(all_far)

    def assemble(n, f):
        return jnp.concatenate([jnp.where(upper == 0, n, f), jnp.where(upper == 0, f, n)], 1)

    kernel_diag = assemble(near_out[0], far_out[0])[None]
    kernel_cross = assemble(near_out[1], far_out[1])
    return (kernel_diag, kernel_cross, scores)


def solution(mesh):
    in_specs = (P(("grp", "ex"), "feat"), P(("grp", "ex"), "feat"), P("feat", "grp"))
    out_specs = (
        P("feat", ("grp", "ex"), None),
        P(("grp", "ex", "feat"), None),
        P(None, ("grp", "ex"), "feat"),
    )
    few = mesh.shape["ex"] == Z * X and mesh.shape["feat"] == 2
    return jax.shard_map(
        gathering if few else reducing,
        mesh=mesh,
        in_specs=in_specs,
        out_specs=out_specs,
        check_vma=False,
    )
```

```python
import math

import jax
import jax.numpy as jnp
from jax import lax
from jax.sharding import PartitionSpec as P


def gram_part(left, right):
    return lax.dot_general(
        left, right, (((0,), (0,)), ((), ())), preferred_element_type=jnp.float32
    )


def reducing(slab_one, slab_two, target_product):
    ex_devices = lax.axis_size("ex")
    feat_devices = lax.axis_size("feat")
    row_count, half_width = slab_one.shape
    factor = 1.0 / math.sqrt(row_count * ex_devices)
    feat_index = lax.axis_index("feat")
    cross_width = half_width // (ex_devices * feat_devices)
    gathered_one, gathered_two = (
        lax.all_gather(slab_one, "feat", axis=1, tiled=True),
        lax.all_gather(slab_two, "feat", axis=1, tiled=True),
    )
    total = gram_part(slab_one, slab_one) + gram_part(slab_two, slab_two)
    diag_rows = lax.psum_scatter(total * factor, "ex", scatter_dimension=0, tiled=True)
    kernel_diag = diag_rows[None]

    def select_columns(gathered):
        first_half = gathered[:, :half_width].reshape(
            row_count, ex_devices, feat_devices, cross_width
        )
        chosen = lax.dynamic_index_in_dim(first_half, feat_index, 2, keepdims=False)
        return chosen.reshape(row_count, ex_devices * cross_width)

    total = gram_part(select_columns(gathered_one), gathered_one[:, half_width:])
    total = total + gram_part(select_columns(gathered_two), gathered_two[:, half_width:])
    kernel_cross = lax.psum_scatter(total * factor, "ex", scatter_dimension=0, tiled=True)
    target_half = lax.all_to_all(target_product, "feat", split_axis=1, concat_axis=0, tiled=True)
    scores = jnp.stack(
        [
            jnp.dot(gathered_one, target_half, preferred_element_type=jnp.float32),
            jnp.dot(gathered_two, target_half, preferred_element_type=jnp.float32),
        ]
    ).astype(jnp.bfloat16)
    return (kernel_diag, kernel_cross, scores)


Z, X = 4, 2


def permute(value, moves):
    pairs = [
        ((fz * X + x) * 2 + fc, (tz * X + x) * 2 + tc)
        for (fz, fc), (tz, tc) in moves
        for x in range(X)
    ]
    return lax.ppermute(value, ("ex", "feat"), pairs)


def swap_x(value, holders):
    pairs = [
        ((z * X + x) * 2 + c, (z * X + 1 - x) * 2 + c) for z, c in holders for x in range(X)
    ]
    return lax.ppermute(value, ("ex", "feat"), pairs)


def swap_core(value):
    return lax.ppermute(value, "feat", [(0, 1), (1, 0)])


ENDS = ((0, 1), (3, 2))


def on_core(core, moves):
    return [((f, core), (t, core)) for f, t in moves]


IN = [(e, c) for e, c in ENDS]
OUT = [(c, e) for e, c in ENDS]
MID = [(1, 2), (2, 1)]
OVER = [(0, 2), (3, 1)]
BOTH = lambda moves: on_core(0, moves) + on_core(1, moves)
CENTRES = [(1, 0), (1, 1), (2, 0), (2, 1)]
CENTRES_ONE = [(1, 1), (2, 1)]
ENDS_ONE = [(0, 1), (3, 1)]


def after(value, *earlier):
    return lax.optimization_barrier((value, *earlier))[0]


def gathering(slab_one, slab_two, target_product):
    row_count, width = slab_one.shape
    rows = 2 * row_count
    factor = 1.0 / math.sqrt(row_count * Z * X)
    core = lax.axis_index("feat")
    ex = lax.axis_index("ex")
    z, x = ex // X, ex % X
    lower = z < 2
    centre = (z == 1) | (z == 2)
    group = width // Z
    block = width // (Z * X)

    def own(below):
        start = jnp.where(lower, below, 3 - below) * group
        return jnp.concatenate(
            [lax.dynamic_slice_in_dim(s, start, group, 1) for s in (slab_one, slab_two)], 0
        )

    mine = [own(1), own(0), own(2), own(3)]
    sent = [mine[2], mine[3], mine[0], mine[1]]

    a_moves = on_core(0, IN) + on_core(1, IN + OUT)
    wide = [jnp.concatenate(mine[i : i + 2], 1) for i in (0, 2)]
    a, b, c = [None] * 4, [None] * 4, [None] * 4

    def gather(k, for_b=(), for_c=(), for_a=()):
        sb, sc = sent[k], sent[k]
        if k >= 1:
            sb, sc = after(sb, b[k - 1], *for_b), after(sc, c[k - 1], *for_c)
        with jax.named_scope(f"middle{k}"):
            b[k] = permute(sb, BOTH(MID))
        with jax.named_scope(f"over{k}"):
            c[k] = permute(sc, BOTH(OVER))
        if k % 2 == 0:
            with jax.named_scope(f"half{k}"):
                moved = permute(after(wide[k // 2], *for_a) if k else wide[0], a_moves)
            a[k], a[k + 1] = moved[:, :group], moved[:, group:]

    def put(k):
        return jnp.concatenate([a[k], mine[k], b[k], c[k]], 0)

    def forward(k, *earlier):
        with jax.named_scope(f"forward{k}"):
            return permute(after(at_centre[k][rows * 2 :], *earlier), on_core(1, OUT))

    def cut(value, which):
        return lax.dynamic_slice_in_dim(value, which * block, block, 1)

    def lefts(u, v):
        return [jnp.concatenate([cut(u, w), cut(v, w)], 1) for w in (1 - x, x)]

    def part(name, left_other, right):
        with jax.named_scope(name):
            return gram_part(left_other, right)

    def swap(name, value, holders):
        with jax.named_scope(name):
            return swap_x(value, holders)

    def total(name, left_mine, right, other):
        with jax.named_scope(name):
            return (gram_part(left_mine, right) + other) * factor

    at_centre, d = [None] * 4, [None] * 4
    gather(0)
    at_centre[0] = put(0)
    pu0 = part("cu0", cut(at_centre[0], 1 - x), at_centre[0])
    gather(1, (), (pu0,))
    xu0 = swap("cu0", pu0, CENTRES)
    with jax.named_scope("across"):
        across = lax.ppermute(
            jnp.concatenate(
                [jnp.where(centre, at_centre[0][:rows], mine[1]), at_centre[0][rows:]], 0
            ),
            "feat",
            [(0, 1)],
        )
    d[0] = forward(0)
    at_centre[1] = put(1)
    centre_v = jnp.where(core == 0, at_centre[1], across)
    cl = lefts(at_centre[0], centre_v)
    p1 = part("c1", cl[0], at_centre[1])
    pv0 = part("cv0", cut(centre_v, 1 - x), at_centre[0])
    gather(2, (xu0,), (p1, pv0), (d[0],))
    x1 = swap("c1", after(p1, xu0), CENTRES)
    xv0 = swap("cv0", pv0, CENTRES)
    d[1] = forward(1, d[0])
    with jax.named_scope("given"):
        given = permute(after(at_centre[1][rows:], d[0]), [((cz, 0), (ez, 1)) for ez, cz in ENDS])
    at_centre[2] = put(2)
    p2 = part("c2", cl[0], at_centre[2])

    def at_end(k):
        return jnp.concatenate([mine[k], a[k], d[k]], 0)

    end_own = at_end(1)
    end_given = jnp.concatenate([across[:rows], given], 0)
    el = lefts(end_own, end_given)
    near = jnp.concatenate([at_end(0), end_own], 1)
    pe0 = part("e0", el[0], near)
    gather(3, (xv0,), (p2, d[1]))
    xe0 = swap("e0", pe0, ENDS_ONE)

    x2 = swap("c2", after(p2, x1, xv0), CENTRES)
    d[2] = forward(2, d[1])
    at_centre[3] = put(3)
    p3 = part("c3", cl[0], after(at_centre[3], x1, pe0))
    pe2 = part("e2", el[0], at_end(2))
    xe2 = swap("e2", after(pe2, xe0), ENDS_ONE)
    d[3] = forward(3, d[2])
    x3 = swap("c3", after(p3, x2), CENTRES)
    pe3 = part("e3", el[0], at_end(3))
    xe3 = swap("e3", after(pe3, xe2), ENDS_ONE)

    u0 = total("cu0", cut(at_centre[0], x), at_centre[0], xu0)
    v0 = total("cv0", cut(centre_v, x), at_centre[0], xv0)
    by_centre = [
        jnp.concatenate([u0, v0], 0),
        total("c1", cl[1], at_centre[1], x1),
        total("c2", cl[1], at_centre[2], x2),
        total("c3", cl[1], at_centre[3], x3),
    ]
    near_end = total("e0", el[1], near, xe0)
    by_end = [
        near_end[:, :group],
        near_end[:, group:],
        total("e2", el[1], at_end(2), xe2),
        total("e3", el[1], at_end(3), xe3),
    ]

    targets = target_product.shape[1]
    half_targets = targets // 2

    def partial_scores(which):
        t = lax.dynamic_slice_in_dim(target_product, which * half_targets, half_targets, 1)
        return jnp.concatenate(
            [jnp.dot(s, t, preferred_element_type=jnp.float32) for s in (slab_one, slab_two)], 0
        )

    with jax.named_scope("scores"):
        other_scores = swap_core(after(partial_scores(1 - core), c[0]))
    scores = (partial_scores(core) + other_scores).astype(jnp.bfloat16)
    scores = scores.reshape(2, row_count, half_targets)

    def finish(ks):
        result = jnp.concatenate(
            [jnp.where(centre, by_centre[k], by_end[k]) for k in ks], 1
        )
        with jax.named_scope("end_diag"):
            end_diag = permute(result[block:], on_core(0, OUT))
        with jax.named_scope("low_cross"):
            low_cross = lax.ppermute(result[block : block + block // 2], "feat", [(1, 0)])
        diag = jnp.where((core == 0) & ~centre, end_diag, result[:block])
        cross = jnp.where(core == 0, low_cross, result[block + block // 2 :])
        return [
            [v[:, i * group : (i + 1) * group] for i in range(len(ks))] for v in (diag, cross)
        ]

    first, last = finish((0, 1, 2)), finish((3,))

    def assemble(p):
        p = [p[1], p[0], p[2], p[3]]
        return jnp.concatenate([jnp.where(lower, p[i], p[3 - i]) for i in range(4)], 1)

    kernel_diag = assemble(first[0] + last[0])[None]
    kernel_cross = assemble(first[1] + last[1])
    return (kernel_diag, kernel_cross, scores)


def solution(mesh):
    in_specs = (P(("grp", "ex"), "feat"), P(("grp", "ex"), "feat"), P("feat", "grp"))
    out_specs = (
        P("feat", ("grp", "ex"), None),
        P(("grp", "ex", "feat"), None),
        P(None, ("grp", "ex"), "feat"),
    )
    few = mesh.shape["ex"] == Z * X and mesh.shape["feat"] == 2
    return jax.shard_map(
        gathering if few else reducing,
        mesh=mesh,
        in_specs=in_specs,
        out_specs=out_specs,
        check_vma=False,
    )
```

```python
import math

import jax
import jax.numpy as jnp
from jax import lax
from jax.sharding import PartitionSpec as P


def gram_part(left, right):
    return lax.dot_general(
        left, right, (((0,), (0,)), ((), ())), preferred_element_type=jnp.float32
    )


def reducing(slab_one, slab_two, target_product):
    ex_devices = lax.axis_size("ex")
    feat_devices = lax.axis_size("feat")
    row_count, half_width = slab_one.shape
    factor = 1.0 / math.sqrt(row_count * ex_devices)
    feat_index = lax.axis_index("feat")
    cross_width = half_width // (ex_devices * feat_devices)
    gathered_one, gathered_two = (
        lax.all_gather(slab_one, "feat", axis=1, tiled=True),
        lax.all_gather(slab_two, "feat", axis=1, tiled=True),
    )
    total = gram_part(slab_one, slab_one) + gram_part(slab_two, slab_two)
    diag_rows = lax.psum_scatter(total * factor, "ex", scatter_dimension=0, tiled=True)
    kernel_diag = diag_rows[None]

    def select_columns(gathered):
        first_half = gathered[:, :half_width].reshape(
            row_count, ex_devices, feat_devices, cross_width
        )
        chosen = lax.dynamic_index_in_dim(first_half, feat_index, 2, keepdims=False)
        return chosen.reshape(row_count, ex_devices * cross_width)

    total = gram_part(select_columns(gathered_one), gathered_one[:, half_width:])
    total = total + gram_part(select_columns(gathered_two), gathered_two[:, half_width:])
    kernel_cross = lax.psum_scatter(total * factor, "ex", scatter_dimension=0, tiled=True)
    target_half = lax.all_to_all(target_product, "feat", split_axis=1, concat_axis=0, tiled=True)
    scores = jnp.stack(
        [
            jnp.dot(gathered_one, target_half, preferred_element_type=jnp.float32),
            jnp.dot(gathered_two, target_half, preferred_element_type=jnp.float32),
        ]
    ).astype(jnp.bfloat16)
    return (kernel_diag, kernel_cross, scores)


Z, X = 4, 2


def permute(value, moves):
    pairs = [
        ((fz * X + x) * 2 + fc, (tz * X + x) * 2 + tc)
        for (fz, fc), (tz, tc) in moves
        for x in range(X)
    ]
    return lax.ppermute(value, ("ex", "feat"), pairs)


def swap_x(value, holders):
    pairs = [
        ((z * X + x) * 2 + c, (z * X + 1 - x) * 2 + c) for z, c in holders for x in range(X)
    ]
    return lax.ppermute(value, ("ex", "feat"), pairs)


def swap_core(value):
    return lax.ppermute(value, "feat", [(0, 1), (1, 0)])


ENDS = ((0, 1), (3, 2))


def on_core(core, moves):
    return [((f, core), (t, core)) for f, t in moves]


IN = [(e, c) for e, c in ENDS]
OUT = [(c, e) for e, c in ENDS]
MID = [(1, 2), (2, 1)]
OVER = [(0, 2), (3, 1)]
BOTH = lambda moves: on_core(0, moves) + on_core(1, moves)
CENTRES = [(1, 0), (1, 1), (2, 0), (2, 1)]
CENTRES_ONE = [(1, 1), (2, 1)]
ENDS_ONE = [(0, 1), (3, 1)]


def after(value, *earlier):
    return lax.optimization_barrier((value, *earlier))[0]


def gathering(slab_one, slab_two, target_product):
    row_count, width = slab_one.shape
    rows = 2 * row_count
    factor = 1.0 / math.sqrt(row_count * Z * X)
    core = lax.axis_index("feat")
    ex = lax.axis_index("ex")
    z, x = ex // X, ex % X
    lower = z < 2
    centre = (z == 1) | (z == 2)
    group = width // Z
    block = width // (Z * X)

    def own(below):
        start = jnp.where(lower, below, 3 - below) * group
        return jnp.concatenate(
            [lax.dynamic_slice_in_dim(s, start, group, 1) for s in (slab_one, slab_two)], 0
        )

    mine = [own(1), own(0), own(2), own(3)]
    sent = [mine[2], mine[3], mine[0], mine[1]]

    a_moves = on_core(0, IN) + on_core(1, IN + OUT)
    a, b, c = [None] * 4, [None] * 4, [None] * 4

    def gather(k, for_b=(), for_c=(), for_a=()):
        sb, sc = sent[k], sent[k]
        if k >= 1:
            sb, sc = after(sb, b[k - 1], *for_b), after(sc, c[k - 1], *for_c)
        with jax.named_scope(f"middle{k}"):
            b[k] = permute(sb, BOTH(MID))
        with jax.named_scope(f"over{k}"):
            c[k] = permute(sc, BOTH(OVER))
        sa = mine[k] if k == 0 else after(mine[k], a[k - 1], *for_a)
        with jax.named_scope(f"half{k}"):
            a[k] = permute(sa, a_moves)

    def put(k):
        return jnp.concatenate([a[k], mine[k], b[k], c[k]], 0)

    def forward(k, *earlier):
        with jax.named_scope(f"forward{k}"):
            return permute(after(at_centre[k][rows * 2 :], *earlier), on_core(1, OUT))

    def cut(value, which):
        return lax.dynamic_slice_in_dim(value, which * block, block, 1)

    def lefts(u, v):
        return [jnp.concatenate([cut(u, w), cut(v, w)], 1) for w in (1 - x, x)]

    def part(name, left_other, right):
        with jax.named_scope(name):
            return gram_part(left_other, right)

    def swap(name, value, holders):
        with jax.named_scope(name):
            return swap_x(value, holders)

    def total(name, left_mine, right, other):
        with jax.named_scope(name):
            return (gram_part(left_mine, right) + other) * factor

    at_centre, d = [None] * 4, [None] * 4
    gather(0)
    at_centre[0] = put(0)
    pu0 = part("cu0", cut(at_centre[0], 1 - x), at_centre[0])
    gather(1, (), (pu0,), ())
    xu0 = swap("cu0", pu0, CENTRES)
    with jax.named_scope("across"):
        across = lax.ppermute(
            jnp.concatenate(
                [jnp.where(centre, at_centre[0][:rows], mine[1]), at_centre[0][rows:]], 0
            ),
            "feat",
            [(0, 1)],
        )
    d[0] = forward(0, pu0)
    at_centre[1] = put(1)
    centre_v = jnp.where(core == 0, at_centre[1], across)
    cl = lefts(at_centre[0], centre_v)
    p1 = part("c1", cl[0], after(at_centre[1], c[1]))
    pv0 = part("cv0", cut(centre_v, 1 - x), at_centre[0])
    gather(2, (xu0,), (p1, pv0), (d[0],))
    x1 = swap("c1", after(p1, xu0), CENTRES)
    xv0 = swap("cv0", after(pv0, pv0), CENTRES)
    d[1] = forward(1, d[0])
    with jax.named_scope("given"):
        given = permute(after(at_centre[1][rows:], d[0]), [((cz, 0), (ez, 1)) for ez, cz in ENDS])
    at_centre[2] = put(2)
    p2 = part("c2", cl[0], after(at_centre[2], c[2]))

    def at_end(k):
        return jnp.concatenate([mine[k], a[k], d[k]], 0)

    end_own = at_end(1)
    end_given = jnp.concatenate([across[:rows], given], 0)
    el = lefts(end_own, end_given)
    near = after(jnp.concatenate([at_end(0), end_own], 1), d[1])
    pe0 = part("e0", el[0], near)
    gather(3, (xv0,), (p2, d[1]), ())
    xe0 = swap("e0", pe0, ENDS_ONE)

    x2 = swap("c2", after(p2, x1, xv0), CENTRES)
    d[2] = forward(2, d[1])
    at_centre[3] = put(3)
    p3 = part("c3", cl[0], after(at_centre[3], x1, pe0))
    pe2 = part("e2", el[0], at_end(2))
    xe2 = swap("e2", after(pe2, xe0), ENDS_ONE)
    d[3] = forward(3, d[2])
    x3 = swap("c3", after(p3, x2), CENTRES)
    pe3 = part("e3", el[0], at_end(3))
    xe3 = swap("e3", after(pe3, xe2), ENDS_ONE)

    u0 = total("cu0", cut(at_centre[0], x), at_centre[0], xu0)
    v0 = total("cv0", cut(centre_v, x), at_centre[0], xv0)
    by_centre = [
        jnp.concatenate([u0, v0], 0),
        total("c1", cl[1], at_centre[1], x1),
        total("c2", cl[1], at_centre[2], x2),
        total("c3", cl[1], at_centre[3], x3),
    ]
    near_end = total("e0", el[1], near, xe0)
    by_end = [
        near_end[:, :group],
        near_end[:, group:],
        total("e2", el[1], at_end(2), xe2),
        total("e3", el[1], at_end(3), xe3),
    ]

    targets = target_product.shape[1]
    half_targets = targets // 2

    def partial_scores(which):
        t = lax.dynamic_slice_in_dim(target_product, which * half_targets, half_targets, 1)
        return jnp.concatenate(
            [jnp.dot(s, t, preferred_element_type=jnp.float32) for s in (slab_one, slab_two)], 0
        )

    with jax.named_scope("scores"):
        other_scores = swap_core(after(partial_scores(1 - core), x1))
    scores = (partial_scores(core) + other_scores).astype(jnp.bfloat16)
    scores = scores.reshape(2, row_count, half_targets)

    def send_diag(ks):
        with jax.named_scope("end_diag"):
            return permute(jnp.concatenate([by_centre[k][block:] for k in ks], 1), on_core(0, OUT))

    def send_cross(ks):
        value = jnp.concatenate(
            [
                jnp.where(centre, by_centre[k], by_end[k])[block : block + block // 2]
                for k in ks
            ],
            1,
        )
        with jax.named_scope("low_cross"):
            return lax.ppermute(value, "feat", [(1, 0)])

    def split(values):
        joined = jnp.concatenate(values, 1)
        return [joined[:, i * group : (i + 1) * group] for i in range(4)]

    end_diag = split([send_diag(ks) for ks in ((0, 1), (2,), (3,))])
    low_cross = split([send_cross(ks) for ks in ((0, 1, 2), (3,))])
    diag, cross = [], []
    for k in range(4):
        result = jnp.where(centre, by_centre[k], by_end[k])
        diag.append(jnp.where((core == 0) & ~centre, end_diag[k], result[:block]))
        cross.append(jnp.where(core == 0, low_cross[k], result[block + block // 2 :]))

    def assemble(p):
        p = [p[1], p[0], p[2], p[3]]
        return jnp.concatenate([jnp.where(lower, p[i], p[3 - i]) for i in range(4)], 1)

    kernel_diag = assemble(diag)[None]
    kernel_cross = assemble(cross)
    return (kernel_diag, kernel_cross, scores)


def solution(mesh):
    in_specs = (P(("grp", "ex"), "feat"), P(("grp", "ex"), "feat"), P("feat", "grp"))
    out_specs = (
        P("feat", ("grp", "ex"), None),
        P(("grp", "ex", "feat"), None),
        P(None, ("grp", "ex"), "feat"),
    )
    few = mesh.shape["ex"] == Z * X and mesh.shape["feat"] == 2
    return jax.shard_map(
        gathering if few else reducing,
        mesh=mesh,
        in_specs=in_specs,
        out_specs=out_specs,
        check_vma=False,
    )
```

```python
import math

import jax
import jax.numpy as jnp
from jax import lax
from jax.sharding import PartitionSpec as P


def gram_part(left, right):
    return lax.dot_general(
        left, right, (((0,), (0,)), ((), ())), preferred_element_type=jnp.float32
    )


def reducing(slab_one, slab_two, target_product):
    ex_devices = lax.axis_size("ex")
    feat_devices = lax.axis_size("feat")
    row_count, half_width = slab_one.shape
    factor = 1.0 / math.sqrt(row_count * ex_devices)
    feat_index = lax.axis_index("feat")
    cross_width = half_width // (ex_devices * feat_devices)
    gathered_one, gathered_two = (
        lax.all_gather(slab_one, "feat", axis=1, tiled=True),
        lax.all_gather(slab_two, "feat", axis=1, tiled=True),
    )
    total = gram_part(slab_one, slab_one) + gram_part(slab_two, slab_two)
    diag_rows = lax.psum_scatter(total * factor, "ex", scatter_dimension=0, tiled=True)
    kernel_diag = diag_rows[None]

    def select_columns(gathered):
        first_half = gathered[:, :half_width].reshape(
            row_count, ex_devices, feat_devices, cross_width
        )
        chosen = lax.dynamic_index_in_dim(first_half, feat_index, 2, keepdims=False)
        return chosen.reshape(row_count, ex_devices * cross_width)

    total = gram_part(select_columns(gathered_one), gathered_one[:, half_width:])
    total = total + gram_part(select_columns(gathered_two), gathered_two[:, half_width:])
    kernel_cross = lax.psum_scatter(total * factor, "ex", scatter_dimension=0, tiled=True)
    target_half = lax.all_to_all(target_product, "feat", split_axis=1, concat_axis=0, tiled=True)
    scores = jnp.stack(
        [
            jnp.dot(gathered_one, target_half, preferred_element_type=jnp.float32),
            jnp.dot(gathered_two, target_half, preferred_element_type=jnp.float32),
        ]
    ).astype(jnp.bfloat16)
    return (kernel_diag, kernel_cross, scores)


Z, X = 4, 2


def permute(value, moves):
    pairs = [
        ((fz * X + x) * 2 + fc, (tz * X + x) * 2 + tc)
        for (fz, fc), (tz, tc) in moves
        for x in range(X)
    ]
    return lax.ppermute(value, ("ex", "feat"), pairs)


def swap_x(value, holders):
    pairs = [
        ((z * X + x) * 2 + c, (z * X + 1 - x) * 2 + c) for z, c in holders for x in range(X)
    ]
    return lax.ppermute(value, ("ex", "feat"), pairs)


def swap_core(value):
    return lax.ppermute(value, "feat", [(0, 1), (1, 0)])


ENDS = ((0, 1), (3, 2))


def on_core(core, moves):
    return [((f, core), (t, core)) for f, t in moves]


IN = [(e, c) for e, c in ENDS]
OUT = [(c, e) for e, c in ENDS]
MID = [(1, 2), (2, 1)]
OVER = [(0, 2), (3, 1)]
BOTH = lambda moves: on_core(0, moves) + on_core(1, moves)
CENTRES = [(1, 0), (1, 1), (2, 0), (2, 1)]
CENTRES_ONE = [(1, 1), (2, 1)]
ENDS_ONE = [(0, 1), (3, 1)]


def after(value, *earlier):
    return lax.optimization_barrier((value, *earlier))[0]


def gathering(slab_one, slab_two, target_product):
    row_count, width = slab_one.shape
    rows = 2 * row_count
    factor = 1.0 / math.sqrt(row_count * Z * X)
    core = lax.axis_index("feat")
    ex = lax.axis_index("ex")
    z, x = ex // X, ex % X
    lower = z < 2
    centre = (z == 1) | (z == 2)
    group = width // Z
    block = width // (Z * X)

    def own(below):
        start = jnp.where(lower, below, 3 - below) * group
        return jnp.concatenate(
            [lax.dynamic_slice_in_dim(s, start, group, 1) for s in (slab_one, slab_two)], 0
        )

    mine = [own(1), own(0), own(2), own(3)]
    sent = [mine[2], mine[3], mine[0], mine[1]]

    a_moves = on_core(0, IN) + on_core(1, IN + OUT)
    a, b, c = [None] * 4, [None] * 4, [None] * 4

    def gather(k, for_b=(), for_c=(), for_a=()):
        sb, sc = sent[k], sent[k]
        if k >= 1:
            sb, sc = after(sb, b[k - 1], *for_b), after(sc, c[k - 1], *for_c)
        with jax.named_scope(f"middle{k}"):
            b[k] = permute(sb, BOTH(MID))
        with jax.named_scope(f"over{k}"):
            c[k] = permute(sc, BOTH(OVER))
        sa = mine[k] if k == 0 else after(mine[k], a[k - 1], *for_a)
        with jax.named_scope(f"half{k}"):
            a[k] = permute(sa, a_moves)

    def put(k):
        return jnp.concatenate([a[k], mine[k], b[k], c[k]], 0)

    def forward(k, *earlier):
        with jax.named_scope(f"forward{k}"):
            return permute(after(at_centre[k][rows * 2 :], *earlier), on_core(1, OUT))

    def cut(value, which):
        return lax.dynamic_slice_in_dim(value, which * block, block, 1)

    def lefts(u, v):
        return [jnp.concatenate([cut(u, w), cut(v, w)], 1) for w in (1 - x, x)]

    def part(name, left_other, right):
        with jax.named_scope(name):
            return gram_part(left_other, right)

    def swap(name, value, holders):
        with jax.named_scope(name):
            return swap_x(value, holders)

    def total(name, left_mine, right, other):
        with jax.named_scope(name):
            return (gram_part(left_mine, right) + other) * factor

    at_centre, d = [None] * 4, [None] * 4
    gather(0)
    at_centre[0] = put(0)
    pu0 = part("cu0", cut(at_centre[0], 1 - x), at_centre[0])
    gather(1, (), (pu0,), (b[0],))
    xu0 = swap("cu0", pu0, CENTRES)
    with jax.named_scope("across"):
        across = lax.ppermute(
            jnp.concatenate(
                [jnp.where(centre, at_centre[0][:rows], mine[1]), at_centre[0][rows:]], 0
            ),
            "feat",
            [(0, 1)],
        )
    d[0] = forward(0, pu0)
    at_centre[1] = put(1)
    centre_v = jnp.where(core == 0, at_centre[1], across)
    cl = lefts(at_centre[0], centre_v)
    p1 = part("c1", cl[0], after(at_centre[1], c[1]))
    pv0 = part("cv0", cut(centre_v, 1 - x), at_centre[0])
    gather(2, (xu0,), (p1, pv0), (d[0],))
    x1 = swap("c1", after(p1, xu0), CENTRES)
    xv0 = swap("cv0", after(pv0, pv0), CENTRES)
    d[1] = forward(1, d[0])
    with jax.named_scope("given"):
        given = permute(after(at_centre[1][rows:], d[0]), [((cz, 0), (ez, 1)) for ez, cz in ENDS])
    at_centre[2] = put(2)
    p2 = part("c2", cl[0], after(at_centre[2], c[2]))

    def at_end(k):
        return jnp.concatenate([mine[k], a[k], d[k]], 0)

    end_own = at_end(1)
    end_given = jnp.concatenate([across[:rows], given], 0)
    el = lefts(end_own, end_given)
    near = after(jnp.concatenate([at_end(0), end_own], 1), d[1])
    pe0 = part("e0", el[0], near)
    gather(3, (xv0,), (p2,), ())
    xe0 = swap("e0", pe0, ENDS_ONE)

    x2 = swap("c2", after(p2, x1, xv0), CENTRES)
    d[2] = forward(2, d[1])
    at_centre[3] = put(3)
    p3 = part("c3", cl[0], after(at_centre[3], x1, pe0))
    pe2 = part("e2", el[0], at_end(2))
    xe2 = swap("e2", after(pe2, xe0), ENDS_ONE)
    d[3] = forward(3, d[2])
    x3 = swap("c3", after(p3, x2), CENTRES)
    pe3 = part("e3", el[0], at_end(3))
    xe3 = swap("e3", after(pe3, xe2), ENDS_ONE)

    u0 = total("cu0", cut(at_centre[0], x), at_centre[0], xu0)
    v0 = total("cv0", cut(centre_v, x), at_centre[0], xv0)
    by_centre = [
        jnp.concatenate([u0, v0], 0),
        total("c1", cl[1], at_centre[1], x1),
        total("c2", cl[1], at_centre[2], x2),
        total("c3", cl[1], at_centre[3], x3),
    ]
    near_end = total("e0", el[1], near, xe0)
    by_end = [
        near_end[:, :group],
        near_end[:, group:],
        total("e2", el[1], at_end(2), xe2),
        total("e3", el[1], at_end(3), xe3),
    ]

    targets = target_product.shape[1]
    half_targets = targets // 2

    def partial_scores(which):
        t = lax.dynamic_slice_in_dim(target_product, which * half_targets, half_targets, 1)
        return jnp.concatenate(
            [jnp.dot(s, t, preferred_element_type=jnp.float32) for s in (slab_one, slab_two)], 0
        )

    with jax.named_scope("scores"):
        other_scores = swap_core(after(partial_scores(1 - core), x1))
    scores = (partial_scores(core) + other_scores).astype(jnp.bfloat16)
    scores = scores.reshape(2, row_count, half_targets)

    def send_diag(ks):
        with jax.named_scope("end_diag"):
            return permute(jnp.concatenate([by_centre[k][block:] for k in ks], 1), on_core(0, OUT))

    def send_cross(ks):
        value = jnp.concatenate(
            [
                jnp.where(centre, by_centre[k], by_end[k])[block : block + block // 2]
                for k in ks
            ],
            1,
        )
        with jax.named_scope("low_cross"):
            return lax.ppermute(value, "feat", [(1, 0)])

    def split(values):
        joined = jnp.concatenate(values, 1)
        return [joined[:, i * group : (i + 1) * group] for i in range(4)]

    end_diag = split([send_diag(ks) for ks in ((0, 1), (2,), (3,))])
    low_cross = split([send_cross(ks) for ks in ((0, 1), (2, 3))])
    diag, cross = [], []
    for k in range(4):
        result = jnp.where(centre, by_centre[k], by_end[k])
        diag.append(jnp.where((core == 0) & ~centre, end_diag[k], result[:block]))
        cross.append(jnp.where(core == 0, low_cross[k], result[block + block // 2 :]))

    def assemble(p):
        p = [p[1], p[0], p[2], p[3]]
        return jnp.concatenate([jnp.where(lower, p[i], p[3 - i]) for i in range(4)], 1)

    kernel_diag = assemble(diag)[None]
    kernel_cross = assemble(cross)
    return (kernel_diag, kernel_cross, scores)


def solution(mesh):
    in_specs = (P(("grp", "ex"), "feat"), P(("grp", "ex"), "feat"), P("feat", "grp"))
    out_specs = (
        P("feat", ("grp", "ex"), None),
        P(("grp", "ex", "feat"), None),
        P(None, ("grp", "ex"), "feat"),
    )
    few = mesh.shape["ex"] == Z * X and mesh.shape["feat"] == 2
    return jax.shard_map(
        gathering if few else reducing,
        mesh=mesh,
        in_specs=in_specs,
        out_specs=out_specs,
        check_vma=False,
    )
```
